32 devices in a mesh: rep: 4 (over y, core), fsdp: 8 (over z, x).
Axes of the slice: x: 2, y: 2, z: 4, core: 2. Of those that a mesh axis runs over, the one named last changes fastest.
Arguments:
- tokens: bfloat16 [8192, 1024], P(('rep', 'fsdp')), may hold values from -6 to 6
- segment_ids: int32 [8192], P(('rep', 'fsdp')), may hold values from 0 to 7, as said below
- positions: int32 [8192], P(('rep', 'fsdp')), may hold values from 0 to 1023, as said below
- attn_gain: bfloat16 [2, 1024], P(None, 'fsdp'), may hold values from 0.099609375 to 1.8984375
- w_qkv: bfloat16 [2, 1024, 3072], P(None, 'fsdp'), may hold values from -0.1875 to 0.1875
- w_out: bfloat16 [2, 1024, 1024], P(None, 'fsdp'), may hold values from -2 to 2
- mlp_gain: bfloat16 [2, 1024], P(None, 'fsdp'), may hold values from 0.099609375 to 1.8984375
- w_in: bfloat16 [2, 1024, 5248], P(None, 'fsdp'), may hold values from -0.1875 to 0.1875
- w_down: bfloat16 [2, 2624, 1024], P(None, 'fsdp'), may hold values from -0.125 to 0.125
- cotangent: bfloat16 [8192, 1024], P(('rep', 'fsdp')), may hold values from -6 to 6
Outputs:
- block_output: bfloat16 [8192, 1024], P(('rep', 'fsdp'))
- grad_tokens: float32 [8192, 1024], P(('rep', 'fsdp'))
- grad_attn_gain: float32 [2, 1024], P(None, 'fsdp')
- grad_w_qkv: float32 [2, 1024, 3072], P(None, 'fsdp')
- grad_w_out: float32 [2, 1024, 1024], P(None, 'fsdp')
- grad_mlp_gain: float32 [2, 1024], P(None, 'fsdp')
- grad_w_in: float32 [2, 1024, 5248], P(None, 'fsdp')
- grad_w_down: float32 [2, 2624, 1024], P(None, 'fsdp')
The draws below stay inside these ranges and needn't reach their ends.
Inputs may be any that keep to these rules, and one draw needn't show every extreme that they name: `segment_ids`: each index of rep holds two sequences of 1024 tokens each, and no value is shared by two sequences. Every device of a group holds a block of the group's first sequence followed by a block of its second; each block has 64 to 192 tokens. Within one sequence each position occurs once; positions start at 0 and rise by one along a sequence's tokens, within a device and from each device to the next along fsdp.
All inputs are finite; a program needn't handle non-finite values.
Results may differ from the reference program's by a relative error of at most 0.023.
Values may be sent and summed in bfloat16 or wider, within the bound.
A program may use at most 320 MiB of HBM per device.

```python
import jax
import jax.numpy as jnp
from jax import lax

D = 1024
HEADS = 16
HEAD_DIM = 64
FF = 2624
HALF_WINDOW = 64
LAYERS = 2
TOK_DEV = 256
SPAN = 8
TOKENS = 8192
N_REP = 4
N_FSDP = 8


def shared_layout(key):
    count_key, label_key, pick_key = jax.random.split(key, 3)
    fewest = TOK_DEV // 4
    most = 3 * TOK_DEV // 4
    pair_count = N_FSDP // 2
    pair_rows = jax.random.randint(count_key, (N_REP, pair_count), fewest, most + 1).astype(jnp.int32)
    pair_rows = pair_rows.at[:, 0].set(most).astype(jnp.int32)
    sides = jnp.stack([pair_rows, TOK_DEV - pair_rows], axis=2).reshape(N_REP, N_FSDP).astype(jnp.int32)
    pick_keys = jax.random.split(pick_key, N_REP)

    def one_group(group_key, group_sides):
        order = jax.random.permutation(group_key, N_FSDP).astype(jnp.int32)
        return jnp.zeros((N_FSDP,), jnp.int32).at[order].set(group_sides)
    first_rows = jax.vmap(one_group)(pick_keys, sides).astype(jnp.int32)
    second_rows = (TOK_DEV - first_rows).astype(jnp.int32)
    first_start = (jnp.cumsum(first_rows, axis=1, dtype=jnp.int32) - first_rows).astype(jnp.int32)
    second_start = (jnp.cumsum(second_rows, axis=1, dtype=jnp.int32) - second_rows).astype(jnp.int32)
    labels = jax.random.permutation(label_key, 2 * N_REP).astype(jnp.int32).reshape(N_REP, 2)
    offset = jnp.arange(TOK_DEV, dtype=jnp.int32)[None, None, :]
    in_first = offset < first_rows[:, :, None]
    segments = jnp.where(in_first, labels[:, 0][:, None, None], labels[:, 1][:, None, None])
    places = jnp.where(in_first, first_start[:, :, None] + offset, second_start[:, :, None] + offset - first_rows[:, :, None])
    return (segments.reshape(-1).astype(jnp.int32), places.reshape(-1).astype(jnp.int32))


def draw_segment_ids(key, part):
    segments, places = shared_layout(key)
    return segments


def draw_positions(key, part):
    segments, places = shared_layout(key)
    return places


def block_levels(own_key, dims, pieces, least, top_value):
    level, own = 1.0, jax.random.fold_in(own_key, 6)
    for dim, shards_of in pieces:
        heights = jnp.exp(jax.random.uniform(jax.random.fold_in(own, dim), (shards_of,), jnp.float32, least / len(pieces), top_value / len(pieces)))
        level = level * jnp.repeat(heights, dims[dim] // shards_of).reshape([-1 if axis == dim else 1 for axis in range(len(dims))])
    return level


def gaussian(key, extent, scale, bound, shards=(), held_as=jnp.bfloat16):
    array = jax.random.normal(key, extent, jnp.float32) * scale
    if len(shards) > 0:
        array = block_levels(key, extent, shards, -0.22, 0.18) * array
    return jnp.clip(array, min=-bound, max=bound).astype(held_as)


def setup_inputs(seed: int = 0) -> dict:
    seeds = jax.random.split(jax.random.key(seed), 11)
    return {
        "tokens": gaussian(seeds[0], (TOKENS, D), 1.0, 6.0, ((0, 32),)),
        "segment_ids": draw_segment_ids(jax.random.fold_in(seeds[10], 71), 0),
        "positions": draw_positions(jax.random.fold_in(seeds[10], 71), 0),
        "attn_gain": jnp.clip(1.0 + 0.18 * jax.random.normal(seeds[3], (LAYERS, D), jnp.float32), 0.099609375, 1.8984375).astype(jnp.bfloat16),
        "w_qkv": gaussian(seeds[4], (LAYERS, D, 3 * D), D ** -0.5, 0.1875, ((1, 8),)),
        "w_out": gaussian(seeds[5], (LAYERS, D, D), (max(D // 128, 1)) ** -0.5, 2.0, ((1, 8),)),
        "mlp_gain": jnp.clip(1.0 + 0.18 * jax.random.normal(seeds[6], (LAYERS, D), jnp.float32), 0.099609375, 1.8984375).astype(jnp.bfloat16),
        "w_in": gaussian(seeds[7], (LAYERS, D, 2 * FF), D ** -0.5, 0.1875, ((1, 8),)),
        "w_down": gaussian(seeds[8], (LAYERS, FF, D), FF ** -0.5, 0.125, ((1, 8),)),
        "cotangent": gaussian(seeds[9], (TOKENS, D), 1.0, 6.0, ((0, 32),)),
    }


LOCAL_THETA = 10000.0
GLOBAL_THETA = 160000.0
MASKED_SCORE = -1e+30
NORM_EPSILON = 1e-05

@jax.custom_vjp
def low(v):
    return lax.optimization_barrier(v.astype(jnp.bfloat16)).astype(jnp.float32)

@jax.custom_vjp
def low_back(v):
    return v

def low_keep(v):
    return (low(v), None)

def low_pass(kept, grad):
    return (grad,)

def back_keep(v):
    return (v, None)

def back_low(kept, grad):
    return (low(grad),)
low.defvjp(low_keep, low_pass)
low_back.defvjp(back_keep, back_low)

def layer_norm(values, gain_row):
    center = values - lax.optimization_barrier(jnp.mean(values, axis=-1, keepdims=True))
    spread = lax.optimization_barrier(jnp.mean(center * center, axis=-1, keepdims=True))
    return center * lax.rsqrt(spread + NORM_EPSILON) * gain_row

def rotate(matrix, places, base_theta):
    row_count = matrix.shape[0]
    shaped = matrix.reshape(row_count, HEADS, HEAD_DIM)
    half_dim = HEAD_DIM // 2
    frequency = jnp.power(base_theta, -2.0 * jnp.arange(half_dim, dtype=jnp.float32) / HEAD_DIM)
    angles = places.astype(jnp.float32)[:, None] * frequency[None, :]
    cosine = jnp.cos(angles)[:, None, :]
    sine_part = jnp.sin(angles)[:, None, :]
    first_half = shaped[..., :half_dim]
    second_half = shaped[..., half_dim:]
    turned = jnp.concatenate([first_half * cosine - second_half * sine_part, second_half * cosine + first_half * sine_part], axis=-1)
    return turned.reshape(row_count, HEADS * HEAD_DIM)

def attend(queries, key_rows, value_rows, segment_ids, positions, reach_span):
    group_rows = N_FSDP * TOK_DEV
    block_rows = min(512, group_rows)
    score_scale = HEAD_DIM ** (-0.5)
    starts = jnp.arange(TOKENS // block_rows, dtype=jnp.int32) * block_rows

    def one_block(start):
        base = start // group_rows * group_rows
        query_block = lax.dynamic_slice_in_dim(queries, start, block_rows, 0).reshape(block_rows, HEADS, HEAD_DIM)
        key_block = lax.dynamic_slice_in_dim(key_rows, base, group_rows, 0).reshape(group_rows, HEADS, HEAD_DIM)
        value_block = lax.dynamic_slice_in_dim(value_rows, base, group_rows, 0).reshape(group_rows, HEADS, HEAD_DIM)
        segment_query = lax.dynamic_slice_in_dim(segment_ids, start, block_rows, 0)
        segment_key = lax.dynamic_slice_in_dim(segment_ids, base, group_rows, 0)
        place_query = lax.dynamic_slice_in_dim(positions, start, block_rows, 0)
        place_key = lax.dynamic_slice_in_dim(positions, base, group_rows, 0)
        scores = jnp.einsum('qhd,khd->hqk', query_block, key_block, precision=lax.Precision.HIGHEST) * score_scale
        scores = low_back(scores)
        allowed = (segment_query[:, None] == segment_key[None, :]) & (jnp.abs(place_query[:, None] - place_key[None, :]) <= reach_span)
        scores = jnp.where(allowed[None], scores, MASKED_SCORE)
        highest = lax.optimization_barrier(jnp.max(scores, axis=-1, keepdims=True))
        raised = jnp.exp(scores - highest)
        soft_weights = low(raised / lax.optimization_barrier(jnp.sum(raised, axis=-1, keepdims=True)))
        outputs = jnp.einsum('hqk,khd->qhd', soft_weights, value_block, precision=lax.Precision.HIGHEST)
        return low(low_back(outputs))
    return lax.map(jax.checkpoint(one_block), starts).reshape(TOKENS, HEADS * HEAD_DIM)

def forward(hidden, segment_ids, positions, attn_gain, w_qkv, w_out, mlp_gain, w_in, w_down):
    for layer_index in range(LAYERS):
        base_theta = LOCAL_THETA if layer_index == 0 else GLOBAL_THETA
        reach_span = HALF_WINDOW if layer_index == 0 else SPAN * TOK_DEV
        normed = low(layer_norm(hidden, attn_gain[layer_index]))
        projected = low_back(jnp.dot(normed, w_qkv[layer_index], precision=lax.Precision.HIGHEST))
        queries = low(rotate(projected[:, :D], positions, base_theta))
        key_rows = low(rotate(projected[:, D:2 * D], positions, base_theta))
        value_rows = low(projected[:, 2 * D:])
        attended = attend(queries, key_rows, value_rows, segment_ids, positions, reach_span)
        middle = hidden + low_back(jnp.dot(attended, w_out[layer_index], precision=lax.Precision.HIGHEST))
        normed_mlp = low(layer_norm(middle, mlp_gain[layer_index]))
        raised = low_back(jnp.dot(normed_mlp, w_in[layer_index], precision=lax.Precision.HIGHEST))
        gated = low(jax.nn.gelu(raised[:, :FF], approximate=False) * raised[:, FF:])
        hidden = middle + low_back(jnp.dot(gated, w_down[layer_index], precision=lax.Precision.HIGHEST))
    return hidden

def reference(tokens, segment_ids, positions, attn_gain, w_qkv, w_out, mlp_gain, w_in, w_down, cotangent):

    def run(hidden, gain_attn, mat_qkv, mat_out, gain_mlp, mat_in, mat_down):
        return forward(hidden, segment_ids, positions, gain_attn, mat_qkv, mat_out, gain_mlp, mat_in, mat_down)
    output, pull_back = jax.vjp(run, tokens.astype(jnp.float32), attn_gain.astype(jnp.float32), w_qkv.astype(jnp.float32), w_out.astype(jnp.float32), mlp_gain.astype(jnp.float32), w_in.astype(jnp.float32), w_down.astype(jnp.float32))
    grads = pull_back(cotangent.astype(jnp.float32))
    return (output.astype(jnp.bfloat16), grads[0], grads[1], grads[2], grads[3], grads[4], grads[5], grads[6])
```

```python
import jax
import jax.numpy as jnp
from jax import lax
from jax.sharding import PartitionSpec as P

D = 1024
HEADS = 16
HEAD_DIM = 64
FF = 2624
HALF_WINDOW = 64
LAYERS = 2


LOCAL_THETA = 10000.0
GLOBAL_THETA = 160000.0
MASKED_SCORE = -1e30
NORM_EPSILON = 1e-05


def shifted(value, axis, steps):
    count = lax.axis_size(axis)
    first, last = (max(0, -steps), min(count, count - steps))
    return lax.ppermute(value, axis, [(source, source + steps) for source in range(first, last)])


def layer_norm(values, gain_row):
    center = values - jnp.mean(values, axis=-1, keepdims=True)
    spread = jnp.mean(center * center, axis=-1, keepdims=True)
    return center * lax.rsqrt(spread + NORM_EPSILON) * gain_row


def rotate(matrix, places, base_theta):
    row_count = matrix.shape[0]
    shaped = matrix.reshape(row_count, HEADS, HEAD_DIM)
    half_dim = HEAD_DIM // 2
    frequency = jnp.power(base_theta, -2.0 * jnp.arange(half_dim, dtype=jnp.float32) / HEAD_DIM)
    angles = places.astype(jnp.float32)[:, None] * frequency[None, :]
    cosine = jnp.cos(angles)[:, None, :]
    sine_part = jnp.sin(angles)[:, None, :]
    first_half = shaped[..., :half_dim]
    second_half = shaped[..., half_dim:]
    turned = jnp.concatenate(
        [
            first_half * cosine - second_half * sine_part,
            second_half * cosine + first_half * sine_part,
        ],
        axis=-1,
    )
    return turned.reshape(row_count, HEADS * HEAD_DIM)


def rotate_back(gradient, places, base_theta):
    turned, pull_back = jax.vjp(lambda rotated_in: rotate(rotated_in, places, base_theta), gradient)
    return pull_back(gradient)[0]


def gelu_gate(raised):
    return jax.nn.gelu(raised[:, :FF], approximate=False) * raised[:, FF:]


def contract_rows(left, right):
    return lax.dot_general(
        left, right, (((0,), (0,)), ((), ())), preferred_element_type=jnp.float32
    )


def contract_cols(left, right):
    return lax.dot_general(
        left, right, (((1,), (1,)), ((), ())), preferred_element_type=jnp.float32
    )


def head_block(matrix, group_index, head_width):
    columns = lax.dynamic_slice_in_dim(
        matrix, group_index * head_width * HEAD_DIM, head_width * HEAD_DIM, 1
    )
    return columns.reshape(matrix.shape[0], head_width, HEAD_DIM)


def merge_heads(stacked):
    return jnp.transpose(stacked, (1, 0, 2)).reshape(stacked.shape[1], HEADS * HEAD_DIM)


def attend_forward(queries, key_rows, value_rows, allowed):
    head_width = min(4, HEADS)
    score_scale = HEAD_DIM ** (-0.5)

    def one_group(group_index):
        query_block = head_block(queries, group_index, head_width)
        key_block = head_block(key_rows, group_index, head_width)
        value_block = head_block(value_rows, group_index, head_width)
        scores = (
            jnp.einsum("qhd,khd->hqk", query_block, key_block, preferred_element_type=jnp.float32)
            * score_scale
        )
        scores = jnp.where(allowed[None], scores, MASKED_SCORE)
        highest = jnp.max(scores, axis=-1, keepdims=True)
        raised = jnp.exp(scores - highest)
        totals = jnp.sum(raised, axis=-1, keepdims=True)
        soft_weights = (raised / totals).astype(jnp.bfloat16)
        outputs = jnp.einsum(
            "hqk,khd->qhd", soft_weights, value_block, preferred_element_type=jnp.float32
        )
        return (
            outputs.reshape(outputs.shape[0], head_width * HEAD_DIM),
            (highest + jnp.log(totals))[..., 0],
        )

    outputs, log_sums = lax.map(one_group, jnp.arange(HEADS // head_width, dtype=jnp.int32))
    return (merge_heads(outputs), log_sums)


def attend_backward(queries, key_rows, value_rows, grad_mixed, log_sums, allowed):
    head_width = min(4, HEADS)
    score_scale = HEAD_DIM ** (-0.5)

    def one_group(carried):
        group_index, group_sums = carried
        query_block = head_block(queries, group_index, head_width)
        key_block = head_block(key_rows, group_index, head_width)
        value_block = head_block(value_rows, group_index, head_width)
        grad_block = head_block(grad_mixed, group_index, head_width)
        scores = (
            jnp.einsum("qhd,khd->hqk", query_block, key_block, preferred_element_type=jnp.float32)
            * score_scale
        )
        scores = jnp.where(allowed[None], scores, MASKED_SCORE)
        soft_weights = jnp.exp(scores - group_sums[..., None])
        grad_soft = jnp.einsum(
            "qhd,khd->hqk", grad_block, value_block, preferred_element_type=jnp.float32
        )
        inner_sum = jnp.sum(soft_weights * grad_soft, axis=-1, keepdims=True)
        grad_scores = (soft_weights * (grad_soft - inner_sum)).astype(jnp.bfloat16)
        grad_query = (
            jnp.einsum("hqk,khd->qhd", grad_scores, key_block, preferred_element_type=jnp.float32)
            * score_scale
        )
        grad_query = grad_query.reshape(grad_query.shape[0], head_width * HEAD_DIM)
        grad_key = (
            jnp.einsum("hqk,qhd->khd", grad_scores, query_block, preferred_element_type=jnp.float32)
            * score_scale
        )
        grad_value = jnp.einsum(
            "hqk,qhd->khd",
            soft_weights.astype(jnp.bfloat16),
            grad_block,
            preferred_element_type=jnp.float32,
        )
        return (
            grad_query,
            grad_key.reshape(grad_key.shape[0], head_width * HEAD_DIM),
            grad_value.reshape(grad_value.shape[0], head_width * HEAD_DIM),
            inner_sum[..., 0],
        )

    results = lax.map(one_group, (jnp.arange(HEADS // head_width, dtype=jnp.int32), log_sums))
    return (merge_heads(results[0]), merge_heads(results[1]), merge_heads(results[2]), results[3])


def swap(value, bit):
    count = lax.axis_size("rep")
    return lax.ppermute(value, "rep", [(source, source ^ bit) for source in range(count)])


def swap_core(value):
    return swap(value, 1)


def swap_plane(value):
    return swap(value, 2)


def ordered(flag, own, other):
    return (jnp.where(flag == 0, own, other), jnp.where(flag == 0, other, own))


def gather_rows(shard, core):
    half = shard.shape[0] // 2
    own = lax.all_gather(
        lax.dynamic_slice_in_dim(shard, core * half, half, 0), "fsdp", axis=0, tiled=True
    )
    low, high = ordered(core, own, swap_core(own))
    width = shard.shape[1]
    pair = [part.reshape(-1, 1, half, width) for part in (low, high)]
    return jnp.concatenate(pair, axis=1).reshape(-1, width)


def gather_columns(shard, core):
    half = shard.shape[1] // 2
    own = lax.all_gather(
        lax.dynamic_slice_in_dim(shard, core * half, half, 1), "fsdp", axis=0, tiled=True
    )
    return jnp.concatenate(ordered(core, own, swap_core(own)), axis=1)


def halve(parts, flag, exchange):
    kept = lax.dynamic_index_in_dim(parts, flag, 1, keepdims=False)
    sent = lax.dynamic_index_in_dim(parts, 1 - flag, 1, keepdims=False)
    return (kept.astype(jnp.float32) + exchange(sent).astype(jnp.float32)).astype(jnp.bfloat16)


def reduce_rows(gradient, core, plane):
    count = lax.axis_size("fsdp")
    rows, width = gradient.shape
    piece = rows // count // 4
    parts = gradient.astype(jnp.bfloat16).reshape(count * 2, 2, piece, width)
    parts = halve(parts, core, swap_core).reshape(count, 2, piece, width)
    parts = halve(parts, plane, swap_plane).reshape(count * piece, width)
    own = lax.psum_scatter(parts, "fsdp", scatter_dimension=0, tiled=True)
    return lax.all_gather(own, "rep", axis=0, tiled=True).astype(jnp.float32)


def halve_columns(value, flag, exchange):
    half = value.shape[1] // 2
    kept = lax.dynamic_slice_in_dim(value, flag * half, half, 1)
    sent = lax.dynamic_slice_in_dim(value, (1 - flag) * half, half, 1)
    return (kept.astype(jnp.float32) + exchange(sent).astype(jnp.float32)).astype(jnp.bfloat16)


def reduce_columns(gradient, core, plane):
    parts = halve_columns(gradient.astype(jnp.bfloat16), core, swap_core)
    parts = halve_columns(parts, plane, swap_plane)
    own = lax.psum_scatter(parts, "fsdp", scatter_dimension=0, tiled=True)
    every = lax.all_gather(own, "rep", axis=0, tiled=False)
    return jnp.concatenate([every[0], every[2], every[1], every[3]], axis=1).astype(jnp.float32)


def on_device(
    tokens, segment_ids, positions, attn_gain, w_qkv, w_out, mlp_gain, w_in, w_down, cotangent
):
    row_count = tokens.shape[0]
    member = lax.axis_index("rep")
    core, plane = (member % 2, member // 2)
    place = lax.axis_index("fsdp")
    hops = -(-HALF_WINDOW // (row_count // 4))
    offsets = [step for step in range(-hops, hops + 1)]
    shard_rows = attn_gain.shape[1]
    half_rows = shard_rows // 2

    gains = jnp.concatenate([attn_gain, mlp_gain], axis=0)
    first = lax.dynamic_slice_in_dim(w_qkv[0], core * half_rows, half_rows, 0)
    gain_block = jnp.pad(gains, ((0, half_rows - 2 * LAYERS), (0, 0)))
    own = lax.all_gather(
        jnp.concatenate([first, gain_block], axis=1), "fsdp", axis=0, tiled=True
    )
    low, high = ordered(core, own[:, : 3 * D], swap_core(own[:, : 3 * D]))
    pair = [part.reshape(-1, 1, half_rows, 3 * D) for part in (low, high)]
    qkv_first = jnp.concatenate(pair, axis=1).reshape(D, 3 * D)
    all_gains = own[:, 3 * D :].reshape(-1, half_rows, shard_rows)[:, : 2 * LAYERS]
    all_gains = jnp.transpose(all_gains, (1, 0, 2)).reshape(2 * LAYERS, D).astype(jnp.float32)

    marks = lax.all_gather(jnp.stack([segment_ids, positions]), "fsdp", axis=1, tiled=True)
    padded = jnp.pad(marks, ((0, 0), (hops * row_count, hops * row_count)), constant_values=-1)
    near = lax.dynamic_slice_in_dim(padded, place * row_count, len(offsets) * row_count, 1)
    allowed_near = (segment_ids[:, None] == near[0][None, :]) & (
        jnp.abs(positions[:, None] - near[1][None, :]) <= HALF_WINDOW
    )
    allowed_all = segment_ids[:, None] == marks[0][None, :]

    out_first = gather_rows(w_out[0], core)
    in_first = gather_rows(w_in[0], core)
    down_first = gather_columns(w_down[0], core)
    both = gather_rows(jnp.concatenate([w_qkv[1], w_out[1]], axis=1), core)
    matrices = (
        (qkv_first, out_first, in_first, down_first),
        (both[:, : 3 * D], both[:, 3 * D :], gather_rows(w_in[1], core), gather_columns(w_down[1], core)),
    )

    hidden = tokens.astype(jnp.float32)
    memory = []
    for layer_index in range(LAYERS):
        base_theta = LOCAL_THETA if layer_index == 0 else GLOBAL_THETA
        mat_qkv, mat_out, mat_in, mat_down = matrices[layer_index]
        normed = layer_norm(hidden, all_gains[layer_index]).astype(jnp.bfloat16)
        projected = jnp.dot(normed, mat_qkv, preferred_element_type=jnp.float32)
        queries = rotate(projected[:, :D], positions, base_theta).astype(jnp.bfloat16)
        pairs = jnp.concatenate(
            [
                rotate(projected[:, D : 2 * D], positions, base_theta).astype(jnp.bfloat16),
                projected[:, 2 * D :].astype(jnp.bfloat16),
            ],
            axis=1,
        )
        if layer_index == 0:
            rows = jnp.concatenate(
                [pairs if step == 0 else shifted(pairs, "fsdp", -step) for step in offsets], axis=0
            )
            allowed = allowed_near
        else:
            rows = lax.all_gather(pairs, "fsdp", axis=0, tiled=True)
            allowed = allowed_all
        key_rows, value_rows = (rows[:, :D], rows[:, D:])
        attended, log_sums = attend_forward(queries, key_rows, value_rows, allowed)
        attended = attended.astype(jnp.bfloat16)
        middle = hidden + jnp.dot(attended, mat_out, preferred_element_type=jnp.float32)
        normed_mlp = layer_norm(middle, all_gains[LAYERS + layer_index]).astype(jnp.bfloat16)
        raised = jnp.dot(normed_mlp, mat_in, preferred_element_type=jnp.float32)
        gated_hidden = gelu_gate(raised).astype(jnp.bfloat16)
        output = middle + jnp.dot(gated_hidden, mat_down, preferred_element_type=jnp.float32)
        memory.append(
            (
                hidden,
                normed,
                queries,
                key_rows,
                value_rows,
                allowed,
                attended,
                log_sums,
                middle,
                normed_mlp,
                raised,
                gated_hidden,
            )
        )
        hidden = output
    grad_hidden = cotangent.astype(jnp.float32)
    owned = [None, None]
    gain_rows = [None] * (2 * LAYERS)
    for layer_index in range(LAYERS - 1, -1, -1):
        base_theta = LOCAL_THETA if layer_index == 0 else GLOBAL_THETA
        (
            layer_input,
            normed,
            queries,
            key_rows,
            value_rows,
            allowed,
            attended,
            log_sums,
            middle,
            normed_mlp,
            raised,
            gated_hidden,
        ) = memory[layer_index]
        mat_qkv, mat_out, mat_in, mat_down = matrices[layer_index]
        grad_branch = grad_hidden.astype(jnp.bfloat16)
        own_down = reduce_columns(contract_rows(gated_hidden, grad_branch), core, plane)
        grad_gated = contract_cols(grad_branch, mat_down)
        unused, pull_gate = jax.vjp(gelu_gate, raised)
        grad_raised = pull_gate(grad_gated)[0].astype(jnp.bfloat16)
        own_in = reduce_rows(contract_rows(normed_mlp, grad_raised), core, plane)
        grad_normed_mlp = contract_cols(grad_raised, mat_in)
        unused, pull_norm = jax.vjp(layer_norm, middle, all_gains[LAYERS + layer_index])
        grad_middle_part, gain_rows[LAYERS + layer_index] = pull_norm(grad_normed_mlp)
        grad_middle = grad_hidden + grad_middle_part
        grad_attn_in = grad_middle.astype(jnp.bfloat16)
        own_out = reduce_rows(contract_rows(attended, grad_attn_in), core, plane)
        grad_mixed = contract_cols(grad_attn_in, mat_out).astype(jnp.bfloat16)
        grad_queries, grad_keys, grad_values, inner = attend_backward(
            queries, key_rows, value_rows, grad_mixed, log_sums, allowed
        )
        pair_grads = jnp.concatenate([grad_keys, grad_values], axis=1)
        if layer_index == 0:
            window_grads = pair_grads.reshape(len(offsets), row_count, 2 * D)
            summed = window_grads[hops]
            for slot, step in enumerate(offsets):
                if step != 0:
                    piece = window_grads[slot].astype(jnp.bfloat16)
                    summed = summed + shifted(piece, "fsdp", step).astype(jnp.float32)
        else:
            summed = lax.psum_scatter(
                pair_grads.astype(jnp.bfloat16), "fsdp", scatter_dimension=0, tiled=True
            ).astype(jnp.float32)
        grad_projected = jnp.concatenate(
            [
                rotate_back(grad_queries, positions, base_theta),
                rotate_back(summed[:, :D], positions, base_theta),
                summed[:, D:],
            ],
            axis=1,
        ).astype(jnp.bfloat16)
        own_qkv = reduce_rows(contract_rows(normed, grad_projected), core, plane)
        grad_normed = contract_cols(grad_projected, mat_qkv)
        unused, pull_first = jax.vjp(layer_norm, layer_input, all_gains[layer_index])
        grad_hidden_part, gain_rows[layer_index] = pull_first(grad_normed)
        grad_hidden = grad_middle + grad_hidden_part
        owned[layer_index] = (own_qkv, own_out, own_in, own_down)
    gain_sums = lax.psum(jnp.stack(gain_rows), ("rep", "fsdp"))
    gain_own = lax.dynamic_slice_in_dim(gain_sums, place * shard_rows, shard_rows, 1)
    grads = [jnp.stack([owned[0][index], owned[1][index]]) for index in range(4)]
    return (
        hidden.astype(jnp.bfloat16),
        grad_hidden,
        gain_own[:LAYERS],
        grads[0],
        grads[1],
        gain_own[LAYERS:],
        grads[2],
        grads[3],
    )


def solution(mesh):
    return jax.shard_map(
        on_device,
        mesh=mesh,
        in_specs=(
            P(("rep", "fsdp"), None),
            P(("rep", "fsdp")),
            P(("rep", "fsdp")),
            P(None, "fsdp"),
            P(None, "fsdp", None),
            P(None, "fsdp", None),
            P(None, "fsdp"),
            P(None, "fsdp", None),
            P(None, "fsdp", None),
            P(("rep", "fsdp"), None),
        ),
        out_specs=(
            P(("rep", "fsdp"), None),
            P(("rep", "fsdp"), None),
            P(None, "fsdp"),
            P(None, "fsdp", None),
            P(None, "fsdp", None),
            P(None, "fsdp"),
            P(None, "fsdp", None),
            P(None, "fsdp", None),
        ),
        check_vma=False,
    )
```

```python
import jax
import jax.numpy as jnp
from jax import lax
from jax.sharding import PartitionSpec as P

D = 1024
HEADS = 16
HEAD_DIM = 64
FF = 2624
HALF_WINDOW = 64
LAYERS = 2


LOCAL_THETA = 10000.0
GLOBAL_THETA = 160000.0
MASKED_SCORE = -1e30
NORM_EPSILON = 1e-05


def shifted(value, axis, steps):
    count = lax.axis_size(axis)
    first, last = (max(0, -steps), min(count, count - steps))
    return lax.ppermute(value, axis, [(source, source + steps) for source in range(first, last)])


def layer_norm(values, gain_row):
    center = values - jnp.mean(values, axis=-1, keepdims=True)
    spread = jnp.mean(center * center, axis=-1, keepdims=True)
    return center * lax.rsqrt(spread + NORM_EPSILON) * gain_row


def rotate(matrix, places, base_theta):
    row_count = matrix.shape[0]
    shaped = matrix.reshape(row_count, HEADS, HEAD_DIM)
    half_dim = HEAD_DIM // 2
    frequency = jnp.power(base_theta, -2.0 * jnp.arange(half_dim, dtype=jnp.float32) / HEAD_DIM)
    angles = places.astype(jnp.float32)[:, None] * frequency[None, :]
    cosine = jnp.cos(angles)[:, None, :]
    sine_part = jnp.sin(angles)[:, None, :]
    first_half = shaped[..., :half_dim]
    second_half = shaped[..., half_dim:]
    turned = jnp.concatenate(
        [
            first_half * cosine - second_half * sine_part,
            second_half * cosine + first_half * sine_part,
        ],
        axis=-1,
    )
    return turned.reshape(row_count, HEADS * HEAD_DIM)


def rotate_back(gradient, places, base_theta):
    turned, pull_back = jax.vjp(lambda rotated_in: rotate(rotated_in, places, base_theta), gradient)
    return pull_back(gradient)[0]


def gelu_gate(raised):
    return jax.nn.gelu(raised[:, :FF], approximate=False) * raised[:, FF:]


def contract_rows(left, right):
    return lax.dot_general(
        left, right, (((0,), (0,)), ((), ())), preferred_element_type=jnp.float32
    )


def contract_cols(left, right):
    return lax.dot_general(
        left, right, (((1,), (1,)), ((), ())), preferred_element_type=jnp.float32
    )


def head_block(matrix, group_index, head_width):
    columns = lax.dynamic_slice_in_dim(
        matrix, group_index * head_width * HEAD_DIM, head_width * HEAD_DIM, 1
    )
    return columns.reshape(matrix.shape[0], head_width, HEAD_DIM)


def merge_heads(stacked):
    return jnp.transpose(stacked, (1, 0, 2)).reshape(stacked.shape[1], HEADS * HEAD_DIM)


def attend_forward(queries, key_rows, value_rows, allowed):
    head_width = min(4, HEADS)
    score_scale = HEAD_DIM ** (-0.5)

    def one_group(group_index):
        query_block = head_block(queries, group_index, head_width)
        key_block = head_block(key_rows, group_index, head_width)
        value_block = head_block(value_rows, group_index, head_width)
        scores = (
            jnp.einsum("qhd,khd->hqk", query_block, key_block, preferred_element_type=jnp.float32)
            * score_scale
        )
        scores = jnp.where(allowed[None], scores, MASKED_SCORE)
        highest = jnp.max(scores, axis=-1, keepdims=True)
        raised = jnp.exp(scores - highest)
        totals = jnp.sum(raised, axis=-1, keepdims=True)
        soft_weights = (raised / totals).astype(jnp.bfloat16)
        outputs = jnp.einsum(
            "hqk,khd->qhd", soft_weights, value_block, preferred_element_type=jnp.float32
        )
        return (
            outputs.reshape(outputs.shape[0], head_width * HEAD_DIM),
            (highest + jnp.log(totals))[..., 0],
        )

    outputs, log_sums = lax.map(one_group, jnp.arange(HEADS // head_width, dtype=jnp.int32))
    return (merge_heads(outputs), log_sums)


def attend_backward(queries, key_rows, value_rows, grad_mixed, log_sums, allowed):
    head_width = min(4, HEADS)
    score_scale = HEAD_DIM ** (-0.5)

    def one_group(carried):
        group_index, group_sums = carried
        query_block = head_block(queries, group_index, head_width)
        key_block = head_block(key_rows, group_index, head_width)
        value_block = head_block(value_rows, group_index, head_width)
        grad_block = head_block(grad_mixed, group_index, head_width)
        scores = (
            jnp.einsum("qhd,khd->hqk", query_block, key_block, preferred_element_type=jnp.float32)
            * score_scale
        )
        scores = jnp.where(allowed[None], scores, MASKED_SCORE)
        soft_weights = jnp.exp(scores - group_sums[..., None])
        grad_soft = jnp.einsum(
            "qhd,khd->hqk", grad_block, value_block, preferred_element_type=jnp.float32
        )
        inner_sum = jnp.sum(soft_weights * grad_soft, axis=-1, keepdims=True)
        grad_scores = (soft_weights * (grad_soft - inner_sum)).astype(jnp.bfloat16)
        grad_query = (
            jnp.einsum("hqk,khd->qhd", grad_scores, key_block, preferred_element_type=jnp.float32)
            * score_scale
        )
        grad_query = grad_query.reshape(grad_query.shape[0], head_width * HEAD_DIM)
        grad_key = (
            jnp.einsum("hqk,qhd->khd", grad_scores, query_block, preferred_element_type=jnp.float32)
            * score_scale
        )
        grad_value = jnp.einsum(
            "hqk,qhd->khd",
            soft_weights.astype(jnp.bfloat16),
            grad_block,
            preferred_element_type=jnp.float32,
        )
        return (
            grad_query,
            grad_key.reshape(grad_key.shape[0], head_width * HEAD_DIM),
            grad_value.reshape(grad_value.shape[0], head_width * HEAD_DIM),
            inner_sum[..., 0],
        )

    results = lax.map(one_group, (jnp.arange(HEADS // head_width, dtype=jnp.int32), log_sums))
    return (merge_heads(results[0]), merge_heads(results[1]), merge_heads(results[2]), results[3])


def swap(value, bit):
    count = lax.axis_size("rep")
    return lax.ppermute(value, "rep", [(source, source ^ bit) for source in range(count)])


def swap_core(value):
    return swap(value, 1)


def swap_plane(value):
    return swap(value, 2)


def ordered(flag, own, other):
    return (jnp.where(flag == 0, own, other), jnp.where(flag == 0, other, own))


def after(value, anchor):
    return lax.optimization_barrier((value, anchor))[0]


def begin_rows(shard, core):
    half = shard.shape[0] // 2
    return lax.all_gather(
        lax.dynamic_slice_in_dim(shard, core * half, half, 0), "fsdp", axis=0, tiled=True
    )


def end_rows(own, core):
    half, width = own.shape[0] // lax.axis_size("fsdp"), own.shape[1]
    pair = [part.reshape(-1, 1, half, width) for part in ordered(core, own, swap_core(own))]
    return jnp.concatenate(pair, axis=1).reshape(-1, width)


def begin_columns(shard, core):
    half = shard.shape[1] // 2
    return lax.all_gather(
        lax.dynamic_slice_in_dim(shard, core * half, half, 1), "fsdp", axis=0, tiled=True
    )


def end_columns(own, core):
    return jnp.concatenate(ordered(core, own, swap_core(own)), axis=1)


def halve(parts, flag, exchange):
    kept = lax.dynamic_index_in_dim(parts, flag, 1, keepdims=False)
    sent = lax.dynamic_index_in_dim(parts, 1 - flag, 1, keepdims=False)
    return (kept.astype(jnp.float32) + exchange(sent).astype(jnp.float32)).astype(jnp.bfloat16)


def quarter_rows(gradient, core, plane):
    count = lax.axis_size("fsdp")
    rows, width = gradient.shape
    piece = rows // count // 4
    parts = gradient.astype(jnp.bfloat16).reshape(count * 2, 2, piece, width)
    parts = halve(parts, core, swap_core).reshape(count, 2, piece, width)
    return halve(parts, plane, swap_plane)


def halve_columns(value, flag, exchange):
    half = value.shape[1] // 2
    kept = lax.dynamic_slice_in_dim(value, flag * half, half, 1)
    sent = lax.dynamic_slice_in_dim(value, (1 - flag) * half, half, 1)
    return (kept.astype(jnp.float32) + exchange(sent).astype(jnp.float32)).astype(jnp.bfloat16)


def quarter_columns(gradient, core, plane, piece):
    parts = halve_columns(gradient.astype(jnp.bfloat16), core, swap_core)
    parts = halve_columns(parts, plane, swap_plane)
    return parts.reshape(lax.axis_size("fsdp"), piece, -1)


def scatter_shares(blocks):
    count, piece = blocks[0].shape[:2]
    joined = jnp.concatenate(blocks, axis=2).reshape(count * piece, -1)
    own = lax.psum_scatter(joined, "fsdp", scatter_dimension=0, tiled=True)
    every = lax.all_gather(own, "rep", axis=0, tiled=False)
    shares, start = [], 0
    for block in blocks:
        shares.append(every[:, :, start : start + block.shape[2]])
        start += block.shape[2]
    return shares


def whole_rows(share):
    return share.reshape(-1, share.shape[2]).astype(jnp.float32)


def whole_columns(share):
    every = share.reshape(4, -1, D // 4)
    return jnp.concatenate([every[0], every[2], every[1], every[3]], axis=1).astype(jnp.float32)


def gain_block(rows, piece):
    split = rows.astype(jnp.bfloat16).reshape(rows.shape[0], lax.axis_size("fsdp"), -1)
    return jnp.pad(jnp.transpose(split, (1, 0, 2)), ((0, 0), (0, piece - rows.shape[0]), (0, 0)))


def on_device(
    tokens, segment_ids, positions, attn_gain, w_qkv, w_out, mlp_gain, w_in, w_down, cotangent
):
    row_count = tokens.shape[0]
    member = lax.axis_index("rep")
    core, plane = (member % 2, member // 2)
    place = lax.axis_index("fsdp")
    hops = -(-HALF_WINDOW // (row_count // 4))
    offsets = [step for step in range(-hops, hops + 1)]
    shard_rows = attn_gain.shape[1]
    half_rows = shard_rows // 2

    marks = jnp.stack([segment_ids, positions // 64, positions % 64]).astype(jnp.bfloat16)
    gains = jnp.concatenate([attn_gain, mlp_gain, marks.reshape(-1, shard_rows)], axis=0)
    first = jnp.concatenate([w_qkv[0], w_out[0]], axis=1)
    first = lax.dynamic_slice_in_dim(first, core * half_rows, half_rows, 0)
    spare = jnp.pad(gains, ((0, half_rows - gains.shape[0]), (0, 0)))
    own = lax.all_gather(
        jnp.concatenate([first, spare], axis=1), "fsdp", axis=0, tiled=True
    )
    both_first = end_rows(own[:, : 4 * D], core)
    small = own[:, 4 * D :].reshape(-1, half_rows, shard_rows)
    all_gains = jnp.transpose(small[:, : 2 * LAYERS], (1, 0, 2))
    all_gains = all_gains.reshape(2 * LAYERS, D).astype(jnp.float32)
    marks = small[:, 2 * LAYERS : gains.shape[0]].reshape(-1, 3, row_count)
    marks = jnp.transpose(marks, (1, 0, 2)).reshape(3, -1).astype(jnp.int32)
    marks = jnp.stack([marks[0], marks[1] * 64 + marks[2]])

    padded = jnp.pad(marks, ((0, 0), (hops * row_count, hops * row_count)), constant_values=-1)
    near = lax.dynamic_slice_in_dim(padded, place * row_count, len(offsets) * row_count, 1)
    allowed_near = (segment_ids[:, None] == near[0][None, :]) & (
        jnp.abs(positions[:, None] - near[1][None, :]) <= HALF_WINDOW
    )
    allowed_all = segment_ids[:, None] == marks[0][None, :]

    began = (
        (None, begin_rows(w_in[0], core), begin_columns(w_down[0], core)),
        (
            begin_rows(jnp.concatenate([w_qkv[1], w_out[1]], axis=1), core),
            begin_rows(w_in[1], core),
            begin_columns(w_down[1], core),
        ),
    )
    matrices = []
    both = both_first

    hidden = tokens.astype(jnp.float32)
    memory = []
    for layer_index in range(LAYERS):
        base_theta = LOCAL_THETA if layer_index == 0 else GLOBAL_THETA
        mat_qkv, mat_out = (both[:, : 3 * D], both[:, 3 * D :])
        normed = layer_norm(hidden, all_gains[layer_index]).astype(jnp.bfloat16)
        projected = jnp.dot(normed, mat_qkv, preferred_element_type=jnp.float32)
        queries = rotate(projected[:, :D], positions, base_theta).astype(jnp.bfloat16)
        pairs = jnp.concatenate(
            [
                rotate(projected[:, D : 2 * D], positions, base_theta).astype(jnp.bfloat16),
                projected[:, 2 * D :].astype(jnp.bfloat16),
            ],
            axis=1,
        )
        if layer_index == 0:
            rows = jnp.concatenate(
                [pairs if step == 0 else shifted(pairs, "fsdp", -step) for step in offsets], axis=0
            )
            allowed = allowed_near
        else:
            rows = lax.all_gather(pairs, "fsdp", axis=0, tiled=True)
            allowed = allowed_all
        key_rows, value_rows = (rows[:, :D], rows[:, D:])
        attended, log_sums = attend_forward(queries, key_rows, value_rows, allowed)
        attended = attended.astype(jnp.bfloat16)
        mat_in = end_rows(after(began[layer_index][1], attended), core)
        middle = hidden + jnp.dot(attended, mat_out, preferred_element_type=jnp.float32)
        normed_mlp = layer_norm(middle, all_gains[LAYERS + layer_index]).astype(jnp.bfloat16)
        mat_down = end_columns(after(began[layer_index][2], normed_mlp), core)
        raised = jnp.dot(normed_mlp, mat_in, preferred_element_type=jnp.float32)
        gated_hidden = gelu_gate(raised).astype(jnp.bfloat16)
        if layer_index + 1 < LAYERS:
            both = end_rows(after(began[layer_index + 1][0], gated_hidden), core)
        matrices.append((mat_qkv, mat_out, mat_in, mat_down))
        output = middle + jnp.dot(gated_hidden, mat_down, preferred_element_type=jnp.float32)
        memory.append(
            (
                hidden,
                normed,
                queries,
                key_rows,
                value_rows,
                allowed,
                attended,
                log_sums,
                middle,
                normed_mlp,
                raised,
                gated_hidden,
            )
        )
        hidden = output
    grad_hidden = cotangent.astype(jnp.float32)
    owned = [None, None]
    gain_rows = [None] * (2 * LAYERS)
    for layer_index in range(LAYERS - 1, -1, -1):
        base_theta = LOCAL_THETA if layer_index == 0 else GLOBAL_THETA
        (
            layer_input,
            normed,
            queries,
            key_rows,
            value_rows,
            allowed,
            attended,
            log_sums,
            middle,
            normed_mlp,
            raised,
            gated_hidden,
        ) = memory[layer_index]
        mat_qkv, mat_out, mat_in, mat_down = matrices[layer_index]
        grad_branch = grad_hidden.astype(jnp.bfloat16)
        own_down = quarter_columns(
            contract_rows(gated_hidden, grad_branch), core, plane, shard_rows // 4
        )
        grad_gated = contract_cols(grad_branch, mat_down)
        unused, pull_gate = jax.vjp(gelu_gate, raised)
        grad_raised = pull_gate(grad_gated)[0].astype(jnp.bfloat16)
        own_in = quarter_rows(contract_rows(normed_mlp, grad_raised), core, plane)
        grad_normed_mlp = contract_cols(grad_raised, mat_in)
        unused, pull_norm = jax.vjp(layer_norm, middle, all_gains[LAYERS + layer_index])
        grad_middle_part, gain_rows[LAYERS + layer_index] = pull_norm(grad_normed_mlp)
        grad_middle = grad_hidden + grad_middle_part
        grad_attn_in = grad_middle.astype(jnp.bfloat16)
        own_out = quarter_rows(contract_rows(attended, grad_attn_in), core, plane)
        grad_mixed = contract_cols(grad_attn_in, mat_out).astype(jnp.bfloat16)
        grad_queries, grad_keys, grad_values, inner = attend_backward(
            queries, key_rows, value_rows, grad_mixed, log_sums, allowed
        )
        pair_grads = jnp.concatenate([grad_keys, grad_values], axis=1)
        if layer_index == 0:
            window_grads = pair_grads.reshape(len(offsets), row_count, 2 * D)
            summed = window_grads[hops]
            for slot, step in enumerate(offsets):
                if step != 0:
                    piece = window_grads[slot].astype(jnp.bfloat16)
                    summed = summed + shifted(piece, "fsdp", step).astype(jnp.float32)
        else:
            summed = lax.psum_scatter(
                pair_grads.astype(jnp.bfloat16), "fsdp", scatter_dimension=0, tiled=True
            )
            summed = after(summed, (own_down, own_in, own_out)).astype(jnp.float32)
        grad_projected = jnp.concatenate(
            [
                rotate_back(grad_queries, positions, base_theta),
                rotate_back(summed[:, :D], positions, base_theta),
                summed[:, D:],
            ],
            axis=1,
        ).astype(jnp.bfloat16)
        own_qkv = quarter_rows(contract_rows(normed, grad_projected), core, plane)
        grad_normed = contract_cols(grad_projected, mat_qkv)
        unused, pull_first = jax.vjp(layer_norm, layer_input, all_gains[layer_index])
        grad_hidden_part, gain_rows[layer_index] = pull_first(grad_normed)
        grad_hidden = grad_middle + grad_hidden_part
        gain_part = gain_block(
            jnp.stack([gain_rows[layer_index], gain_rows[LAYERS + layer_index]]), shard_rows // 4
        )
        if layer_index == 0:
            wide = scatter_shares([own_down, own_in, own_out])
            wide = wide + scatter_shares([own_qkv, gain_part])
        else:
            wide = scatter_shares([own_down, own_in, own_out, own_qkv, gain_part])
        owned[layer_index] = (
            whole_rows(wide[3]),
            whole_rows(wide[2]),
            whole_rows(wide[1]),
            whole_columns(wide[0]),
            jnp.sum(wide[4][:, :2].astype(jnp.float32), axis=0),
        )
    grads = [jnp.stack([owned[0][index], owned[1][index]]) for index in range(5)]
    return (
        hidden.astype(jnp.bfloat16),
        grad_hidden,
        grads[4][:, 0],
        grads[0],
        grads[1],
        grads[4][:, 1],
        grads[2],
        grads[3],
    )


def solution(mesh):
    return jax.shard_map(
        on_device,
        mesh=mesh,
        in_specs=(
            P(("rep", "fsdp"), None),
            P(("rep", "fsdp")),
            P(("rep", "fsdp")),
            P(None, "fsdp"),
            P(None, "fsdp", None),
            P(None, "fsdp", None),
            P(None, "fsdp"),
            P(None, "fsdp", None),
            P(None, "fsdp", None),
            P(("rep", "fsdp"), None),
        ),
        out_specs=(
            P(("rep", "fsdp"), None),
            P(("rep", "fsdp"), None),
            P(None, "fsdp"),
            P(None, "fsdp", None),
            P(None, "fsdp", None),
            P(None, "fsdp"),
            P(None, "fsdp", None),
            P(None, "fsdp", None),
        ),
        check_vma=False,
    )
```
